512 devices in a mesh: cand: 16 (over x, z_lo), prompt: 4 (over z_hi, core), tensor: 8 (over y).
Axes of the slice: x: 4, y: 8, z: 8 (z_hi: 2, z_lo: 4; z = z_hi * 4 + z_lo), core: 2. Of those that a mesh axis runs over, the one named last changes fastest.
Arguments:
- owner_index: int32 [4], P('prompt'), may hold values from 0 to 15
- suffix_lengths: int32 [4, 16], P('prompt', 'cand'), may hold values from 64 to 256, as said below
- queries: bfloat16 [4, 4096, 8192], P('prompt', 'cand', 'tensor'), may hold values from -15 to 15
- suffix_kv: bfloat16 [2, 4, 4096, 1024], P(None, 'prompt', 'cand', 'tensor'), may hold values from -6 to 6
- prompt_cache: bfloat16 [2, 4, 16, 4096, 1024], P(None, 'prompt', 'cand', None, 'tensor'), may hold values from -6 to 6
- out_weight: bfloat16 [8192, 4096], P('tensor', 'prompt'), may hold values from -0.09375 to 0.09375
Outputs:
- projected: bfloat16 [4, 4096, 4096], P(None, 'cand', ('prompt', 'tensor'))
The draws below stay inside these ranges and needn't reach their ends.
Inputs may be any that keep to these rules, and one draw needn't show every extreme that they name: `suffix_lengths`: the first candidate of every prompt has all 256 suffix tokens live.
All inputs are finite; a program needn't handle non-finite values.
Results may differ from the reference program's by a relative error of at most 0.0057.
Values may be sent and summed in bfloat16 or wider, within the bound.
No kernel may reach another device: no remote copies, remote signals or barrier semaphores. Data moves between devices by JAX's collectives and lax.ppermute only.
A program may use at most 64 MiB of HBM per device.

```python
import math
import jax
import jax.numpy as jnp
from jax import lax

HQ = 64
KVH = 8
HD = 128
DOUT = 4096
PLEN = 4096
SUF = 256
CANDS = 16
N_CAND = 16
N_PROMPT = 4


def draw_suffix_lengths(key, part):
    key = jax.random.fold_in(key, 3)
    lengths = jax.random.randint(key, (N_PROMPT, CANDS), SUF // 4, SUF + 1, jnp.int32)
    return lengths.at[:, 0].set(SUF)


def draw_queries(key, part):
    key = jax.random.fold_in(key, 7)
    draw_shape = (N_PROMPT, CANDS * SUF, HQ * HD)
    sampled = jnp.clip(2.5 * jax.random.normal(key, draw_shape, jnp.float32), -15.0, 15.0)
    return sampled.astype(jnp.bfloat16)


def draw_prompt_cache(key, part):
    key = jax.random.fold_in(key, 5)
    draw_shape = (2, N_PROMPT, N_CAND, PLEN, KVH * HD)
    sampled = jnp.clip(jax.random.normal(key, draw_shape, jnp.float32), -6.0, 6.0)
    return sampled.astype(jnp.bfloat16)


def with_ends(result, rng, least, high):
    longest = result.shape.index(max(result.shape))
    spots = []
    for shift in (0, 1):
        where = [jax.random.randint(jax.random.fold_in(rng, axis), (), 0, length) for axis, length in enumerate(result.shape)]
        where[longest] = (where[longest] + shift) % result.shape[longest]
        spots.append(tuple(where))
    return result.at[spots[0]].set(least).at[spots[1]].set(high)


def spiked(result, stream_key, source, target, parts, factor):
    def block_of(dim):
        return (jnp.arange(result.shape[dim]) // (result.shape[dim] // parts)).reshape((-1,) + (1,) * (result.ndim - 1 - dim))

    near = jax.random.permutation(stream_key, parts)[block_of(target)]
    second = (block_of(target) + parts // 2) % parts
    return jnp.where((block_of(source) == near) | (block_of(source) == second), factor * result, result)


def shard_levels(key, shape, split, smallest, high):
    def one(axis_at, blocks):
        steps = jax.random.uniform(jax.random.fold_in(jax.random.fold_in(key, 6), axis_at), (blocks,), jnp.float32, smallest / len(split), high / len(split))
        return jnp.repeat(jnp.exp(steps), shape[axis_at] // blocks).reshape((-1,) + (1,) * (len(shape) - axis_at - 1))

    level = one(*split[0])
    for cut in split[1:]:
        level = level * one(*cut)
    return level


def normal_values(stream_key, extent, spread, most, split=(), kind=jnp.bfloat16):
    factor_of = shard_levels(stream_key, extent, split, -0.22, 0.18) if split else 1.0
    values = jax.random.normal(stream_key, extent, jnp.float32) * spread * factor_of
    return jnp.minimum(jnp.maximum(values, -most), most).astype(kind)


def gaussian_with(key, extent, width, limit, cuts, heavy, kind=jnp.bfloat16):
    drawn = width * jax.random.normal(key, extent, jnp.float32)
    if cuts:
        drawn = drawn * shard_levels(key, extent, cuts, -0.22, 0.18)
    return jnp.clip(spiked(drawn, jax.random.fold_in(key, 3), *heavy), -limit, limit).astype(kind)


def setup_inputs(seed: int = 0) -> dict:
    key_of = jax.random.split(jax.random.key(seed), 7)
    owner_index = with_ends(jax.random.randint(key_of[0], (N_PROMPT,), 0, N_CAND), jax.random.fold_in(key_of[0], 1), 0, N_CAND - 1).astype(jnp.int32)
    suffix_lengths = draw_suffix_lengths(jax.random.fold_in(key_of[6], 71), 0)
    queries = draw_queries(jax.random.fold_in(key_of[6], 71), 0)
    suffix_kv = normal_values(key_of[3], (2, N_PROMPT, CANDS * SUF, KVH * HD), 1.0, 6.0, ((1, 4), (2, 16), (3, 8)))
    prompt_cache = draw_prompt_cache(jax.random.fold_in(key_of[6], 71), 0)
    out_weight = gaussian_with(key_of[5], (HQ * HD, DOUT), (HQ * HD) ** -0.5, 0.09375, ((0, 8), (1, 4)), (0, 1, 8, 2.0))
    return dict(owner_index=owner_index, suffix_lengths=suffix_lengths, queries=queries, suffix_kv=suffix_kv, prompt_cache=prompt_cache, out_weight=out_weight)


def attend(query_rows, key_rows, value_rows, length):
    row_count = query_rows.shape[0]
    key_count = key_rows.shape[0]
    kv_count = key_rows.shape[1] // HD
    group_size = HQ // KVH
    score_scale = 1.0 / math.sqrt(HD)
    query_heads = query_rows.astype(jnp.float32).reshape(row_count, kv_count, group_size, HD)
    query_heads = query_heads.transpose(1, 2, 0, 3).reshape(kv_count, group_size * row_count, HD)
    key_heads = key_rows.astype(jnp.float32).reshape(key_count, kv_count, HD).transpose(1, 0, 2)
    value_heads = value_rows.astype(jnp.float32).reshape(key_count, kv_count, HD).transpose(1, 0, 2)
    scores = jnp.einsum('hqd,hkd->hqk', query_heads, key_heads) * score_scale
    position = jnp.arange(group_size * row_count, dtype=jnp.int32) % row_count
    column = jnp.arange(key_count, dtype=jnp.int32) - (key_count - row_count)
    allowed = (column[None, :] < 0) | (column[None, :] <= position[:, None]) & (column[None, :] < length)
    scores = jnp.where(allowed[None], scores, -1e+30)
    row_max = lax.optimization_barrier(jnp.max(scores, axis=-1, keepdims=True))
    exponent = jnp.exp(scores - row_max)
    weights = (exponent / lax.optimization_barrier(jnp.sum(exponent, axis=-1, keepdims=True))).astype(jnp.bfloat16)
    produced = jnp.einsum('hqk,hkd->hqd', weights.astype(jnp.float32), value_heads).astype(jnp.bfloat16)
    produced = produced.reshape(kv_count, group_size, row_count, HD).transpose(2, 0, 1, 3)
    return produced.reshape(row_count, kv_count * group_size * HD)

def reference(owner_index, suffix_lengths, queries, suffix_kv, prompt_cache, out_weight):
    results = []
    for prompt_id in range(N_PROMPT):
        prompt_slot = lax.dynamic_index_in_dim(prompt_cache[:, prompt_id], owner_index[prompt_id], axis=1, keepdims=False)

        def per_candidate(candidate):
            start_index = (candidate * SUF).astype(jnp.int32)
            query_rows = lax.dynamic_slice_in_dim(queries[prompt_id], start_index, SUF, 0)
            suffix_part = lax.dynamic_slice_in_dim(suffix_kv[:, prompt_id], start_index, SUF, 1)
            key_rows = jnp.concatenate([prompt_slot[0], suffix_part[0]], axis=0)
            value_rows = jnp.concatenate([prompt_slot[1], suffix_part[1]], axis=0)
            return attend(query_rows, key_rows, value_rows, suffix_lengths[prompt_id, candidate])
        attended = lax.map(per_candidate, jnp.arange(CANDS, dtype=jnp.int32))
        attended = attended.reshape(CANDS * SUF, HQ * HD)
        results.append(jnp.dot(attended, out_weight, preferred_element_type=jnp.float32).astype(jnp.bfloat16))
    return jnp.stack(results)
```

```python
import math

import jax
import jax.numpy as jnp
from jax import lax
from jax.experimental import pallas as pl
from jax.experimental.pallas import tpu as pltpu
from jax.sharding import PartitionSpec as P

HD = 128
SUF = 256
NX = 4
NZ = 4
GROUP = 8
EXP2_SCALE = math.log2(math.e) / math.sqrt(HD)
MASKED = -1e30


def cand_pairs(f):
    pairs = []
    for x in range(NX):
        for z in range(NZ):
            tx, tz = f(x, z)
            pairs.append((x * NZ + z, (tx % NX) * NZ + tz))
    return pairs


def ring_pairs(n, shift):
    return [(i, (i + shift) % n) for i in range(n)]


SCATTER_GROUPS = [
    [x * NZ + 2 * pair + zi for zi in range(2) for x in range(NX)] for pair in range(2)
]


def dot_t(a, b):
    return lax.dot_general(a, b, (((1,), (1,)), ((), ())), preferred_element_type=jnp.float32)


def dot_n(a, b):
    return lax.dot_general(a, b, (((1,), (0,)), ((), ())), preferred_element_type=jnp.float32)


def with_ones(values):
    return jnp.concatenate([values, jnp.ones_like(values)], axis=1)


def attention_kernel(n_blocks, has_suffix, has_state, last, heads, scalar_ref, *refs):
    refs = list(refs)
    q_ref = refs.pop(0)
    block_refs = [(refs.pop(0), refs.pop(0)) for _ in range(n_blocks)]
    suffix_ref = refs.pop(0) if has_suffix else None
    state_refs = [refs.pop(0) for _ in range(3)] if has_state else None
    outs = refs
    rows = q_ref.shape[0]
    keys_first = scalar_ref[0] == 1
    keys = [jnp.where(keys_first, a[...], b[...]) for a, b in block_refs]
    values = [with_ones(jnp.where(keys_first, b[...], a[...])) for a, b in block_refs]
    if has_suffix:
        keys.append(suffix_ref[0])
        values.append(with_ones(suffix_ref[1]))
        row = lax.broadcasted_iota(jnp.int32, (rows, rows), 0)
        col = lax.broadcasted_iota(jnp.int32, (rows, rows), 1)
        allowed = (col <= row) & (col < scalar_ref[1])
    for h in range(heads):
        lanes = pl.ds(h * HD, HD)
        query = q_ref[:, lanes]
        scores = [dot_t(query, k) * EXP2_SCALE for k in keys]
        if has_suffix:
            scores[-1] = jnp.where(allowed, scores[-1], MASKED)
        row_max = scores[0].max(axis=1, keepdims=True)
        for s in scores[1:]:
            row_max = jnp.maximum(row_max, s.max(axis=1, keepdims=True))
        if has_state:
            old_max = state_refs[1][:, lanes]
            new_max = jnp.maximum(old_max, row_max)
            row_max = new_max[:, :1]
        total = None
        for s, v in zip(scores, values):
            weights = jnp.exp2(s - row_max).astype(jnp.bfloat16)
            part = dot_n(weights, v)
            total = part if total is None else total + part
        acc, denom = total[:, :HD], total[:, HD:]
        if has_state:
            alpha = jnp.exp2(old_max - new_max)
            acc = acc + alpha * state_refs[0][:, lanes]
            denom = denom + alpha * state_refs[2][:, lanes]
        if last:
            outs[0][:, lanes] = (acc / denom).astype(jnp.bfloat16)
        else:
            outs[0][:, lanes] = acc
            outs[1][:, lanes] = jnp.broadcast_to(row_max, (rows, HD))
            outs[2][:, lanes] = denom


def attend(scalars, query_rows, blocks, suffix=None, state=None, last=False):
    rows, width = query_rows.shape
    heads = width // HD
    operands = [query_rows]
    for block in blocks:
        operands.extend(block)
    key_count = sum(a.shape[0] for a, _ in blocks)
    if suffix is not None:
        operands.append(suffix)
        key_count += suffix.shape[1]
    if state is not None:
        operands.extend(state)
    vmem = pl.BlockSpec(memory_space=pltpu.VMEM)
    if last:
        out_shape = [jax.ShapeDtypeStruct((rows, width), jnp.bfloat16)]
    else:
        out_shape = [jax.ShapeDtypeStruct((rows, width), jnp.float32)] * 3
    out = pl.pallas_call(
        lambda *refs: attention_kernel(
            len(blocks), suffix is not None, state is not None, last, heads, *refs
        ),
        out_shape=out_shape,
        in_specs=[pl.BlockSpec(memory_space=pltpu.SMEM)] + [vmem] * len(operands),
        out_specs=[vmem] * len(out_shape),
        compiler_params=pltpu.CompilerParams(vmem_limit_bytes=40 * 1024 * 1024),
        cost_estimate=pl.CostEstimate(
            flops=8 * rows * heads * key_count * HD,
            bytes_accessed=2**22,
            transcendentals=rows * heads * key_count,
        ),
    )(scalars, *operands)
    return out[0] if last else out


def spread_piece(prompt_kv, owner):
    me = lax.axis_index("cand")
    z = me % NZ
    owner_x, owner_z = owner // NZ, owner % NZ
    pieces = prompt_kv.reshape(GROUP, -1, HD)
    arrived = lax.all_to_all(
        pieces, "cand", split_axis=0, concat_axis=0, axis_index_groups=SCATTER_GROUPS
    )
    piece = lax.dynamic_index_in_dim(
        arrived, (owner_z % 2) * NX + owner_x, axis=0, keepdims=False
    )
    crossed = lax.ppermute(piece, "cand", cand_pairs(lambda x, z: (x, z ^ 2)))
    return jnp.where(owner_z // 2 == z // 2, piece, crossed)


def projection_kernel(core_ref, rows_ref, own_ref, other_ref, out_ref):
    rows = rows_ref[...]
    core = core_ref[0]
    n = own_ref.shape[1] // HD
    for i in range(n):
        lanes = pl.ds(i * HD, HD)
        both = dot_n(rows, jnp.concatenate([own_ref[:, lanes], other_ref[:, lanes]], axis=1))
        both = both.astype(jnp.bfloat16)
        out_ref[core * n + i] = both[:, :HD]
        out_ref[(1 - core) * n + i] = both[:, HD:]


def project(rows, own, other):
    count, depth = rows.shape
    width = own.shape[1]
    core = (lax.axis_index("prompt") % 2).astype(jnp.int32).reshape(1)
    vmem = pl.BlockSpec(memory_space=pltpu.VMEM)
    return pl.pallas_call(
        projection_kernel,
        out_shape=jax.ShapeDtypeStruct((2 * width // HD, count, HD), jnp.bfloat16),
        in_specs=[pl.BlockSpec(memory_space=pltpu.SMEM)] + [vmem] * 3,
        out_specs=vmem,
        compiler_params=pltpu.CompilerParams(vmem_limit_bytes=32 * 1024 * 1024),
        cost_estimate=pl.CostEstimate(
            flops=80 * width * count * depth,
            bytes_accessed=4 * depth * width,
            transcendentals=0,
        ),
    )(core, rows, own, other)


def exchange(products):
    n = products.shape[0]
    return lax.all_to_all(
        products,
        ("prompt", "tensor"),
        split_axis=0,
        concat_axis=0,
        axis_index_groups=[list(range(n)), list(range(n, 2 * n))],
    )


def add_up(terms):
    n, rows, columns = terms.shape
    terms = terms.reshape(2, n // 2, rows, columns).astype(jnp.float32)
    return terms.sum(axis=1).astype(jnp.bfloat16)


def swap(value, bit):
    return lax.ppermute(value, "prompt", [(p, p ^ bit) for p in range(4)])


def move(value, shift):
    return lax.ppermute(value, "cand", cand_pairs(lambda x, z: (x + shift, z)))


def body(owner_index, suffix_lengths, queries, suffix_kv, prompt_cache, out_weight):
    query_rows = queries[0]
    weights = [out_weight, swap(out_weight, 1)]
    piece = spread_piece(prompt_cache[:, 0, 0], owner_index[0])
    keys_first = (lax.axis_index("cand") % 2 == 0).astype(jnp.int32)
    scalars = jnp.stack([keys_first, suffix_lengths[0, 0]])
    other = lax.ppermute(piece, "cand", cand_pairs(lambda x, z: (x, z ^ 1)))
    left, right = [move(piece, 1)], [move(piece, -1)]
    left.append(move(other, 1))
    right.append(move(other, -1))
    across = [move(right[0], -1), move(left[1], 1)]
    state = attend(scalars, query_rows, [(piece, other)], suffix=suffix_kv[:, 0])
    state = attend(scalars, query_rows, [left, right], state=state)
    attended = attend(scalars, query_rows, [across], state=state, last=True)
    far_rows = swap(attended, 2)
    near = add_up(exchange(project(attended, *weights)))
    far = add_up(exchange(project(far_rows, *weights)))
    first = lax.axis_index("prompt") < 2
    return jnp.concatenate([jnp.where(first, near, far), jnp.where(first, far, near)])


def solution(mesh):
    in_specs = (
        P("prompt"),
        P("prompt", "cand"),
        P("prompt", "cand", "tensor"),
        P(None, "prompt", "cand", "tensor"),
        P(None, "prompt", "cand", None, "tensor"),
        P("tensor", "prompt"),
    )
    out_specs = P(None, "cand", ("prompt", "tensor"))
    return jax.shard_map(body, mesh=mesh, in_specs=in_specs, out_specs=out_specs, check_vma=False)
```

```python
import math

import jax
import jax.numpy as jnp
from jax import lax
from jax.experimental import pallas as pl
from jax.experimental.pallas import tpu as pltpu
from jax.sharding import PartitionSpec as P

HD = 128
SUF = 256
NX = 4
NZ = 4
GROUP = 8
CHUNK = 512
EXP2_SCALE = math.log2(math.e) / math.sqrt(HD)
MASKED = -1e30


def cand_pairs(f):
    pairs = []
    for x in range(NX):
        for z in range(NZ):
            tx, tz = f(x, z)
            pairs.append((x * NZ + z, (tx % NX) * NZ + tz))
    return pairs


def ring_pairs(n, shift):
    return [(i, (i + shift) % n) for i in range(n)]


SCATTER_GROUPS = [
    [x * NZ + 2 * pair + zi for zi in range(2) for x in range(NX)] for pair in range(2)
]


def dot_t(a, b):
    return lax.dot_general(a, b, (((1,), (1,)), ((), ())), preferred_element_type=jnp.float32)


def dot_n(a, b):
    return lax.dot_general(a, b, (((1,), (0,)), ((), ())), preferred_element_type=jnp.float32)


def with_ones(values):
    return jnp.concatenate([values, jnp.ones_like(values)], axis=1)


def attention_kernel(n_blocks, has_suffix, has_state, last, heads, scalar_ref, *refs):
    refs = list(refs)
    q_ref = refs.pop(0)
    block_refs = [(refs.pop(0), refs.pop(0)) for _ in range(n_blocks)]
    suffix_ref = refs.pop(0) if has_suffix else None
    state_refs = [refs.pop(0) for _ in range(3)] if has_state else None
    outs = refs
    rows = q_ref.shape[0]
    keys_first = scalar_ref[0] == 1
    keys, values = [], []
    for a, b in block_refs:
        for start in range(0, a.shape[0], CHUNK):
            chunk = pl.ds(start, CHUNK)
            keys.append(jnp.where(keys_first, a[chunk], b[chunk]))
            values.append(with_ones(jnp.where(keys_first, b[chunk], a[chunk])))
    if has_suffix:
        keys.append(suffix_ref[0])
        values.append(with_ones(suffix_ref[1]))
        row = lax.broadcasted_iota(jnp.int32, (rows, rows), 0)
        col = lax.broadcasted_iota(jnp.int32, (rows, rows), 1)
        allowed = (col <= row) & (col < scalar_ref[1])

    def score(lanes):
        query = q_ref[:, lanes]
        scores = [dot_t(query, k) * EXP2_SCALE for k in keys]
        if has_suffix:
            scores[-1] = jnp.where(allowed, scores[-1], MASKED)
        return lanes, scores

    def weigh(lanes, scores):
        row_max = scores[0].max(axis=1, keepdims=True)
        for s in scores[1:]:
            row_max = jnp.maximum(row_max, s.max(axis=1, keepdims=True))
        if has_state:
            old_max = state_refs[1][:, lanes]
            new_max = jnp.maximum(old_max, row_max)
            row_max = new_max[:, :1]
        total = None
        for s, v in zip(scores, values):
            weights = jnp.exp2(s - row_max).astype(jnp.bfloat16)
            part = dot_n(weights, v)
            total = part if total is None else total + part
        acc, denom = total[:, :HD], total[:, HD:]
        if has_state:
            alpha = jnp.exp2(old_max - new_max)
            acc = acc + alpha * state_refs[0][:, lanes]
            denom = denom + alpha * state_refs[2][:, lanes]
        if last:
            outs[0][:, lanes] = (acc / denom).astype(jnp.bfloat16)
        else:
            outs[0][:, lanes] = acc
            outs[1][:, lanes] = jnp.broadcast_to(row_max, (rows, HD))
            outs[2][:, lanes] = denom

    pending = None
    for h in range(heads):
        scored = score(pl.ds(h * HD, HD))
        if pending is not None:
            weigh(*pending)
        pending = scored
    weigh(*pending)


def attend(scalars, query_rows, blocks, suffix=None, state=None, last=False):
    rows, width = query_rows.shape
    heads = width // HD
    operands = [query_rows]
    for block in blocks:
        operands.extend(block)
    key_count = sum(a.shape[0] for a, _ in blocks)
    if suffix is not None:
        operands.append(suffix)
        key_count += suffix.shape[1]
    if state is not None:
        operands.extend(state)
    vmem = pl.BlockSpec(memory_space=pltpu.VMEM)
    if last:
        out_shape = [jax.ShapeDtypeStruct((rows, width), jnp.bfloat16)]
    else:
        out_shape = [jax.ShapeDtypeStruct((rows, width), jnp.float32)] * 3
    out = pl.pallas_call(
        lambda *refs: attention_kernel(
            len(blocks), suffix is not None, state is not None, last, heads, *refs
        ),
        out_shape=out_shape,
        in_specs=[pl.BlockSpec(memory_space=pltpu.SMEM)] + [vmem] * len(operands),
        out_specs=[vmem] * len(out_shape),
        compiler_params=pltpu.CompilerParams(vmem_limit_bytes=40 * 1024 * 1024),
        cost_estimate=pl.CostEstimate(
            flops=8 * rows * heads * key_count * HD,
            bytes_accessed=2**22,
            transcendentals=rows * heads * key_count,
        ),
    )(scalars, *operands)
    return out[0] if last else out


def spread_piece(prompt_kv, owner):
    me = lax.axis_index("cand")
    z = me % NZ
    owner_x, owner_z = owner // NZ, owner % NZ
    pieces = prompt_kv.reshape(GROUP, -1, HD)
    arrived = lax.all_to_all(
        pieces, "cand", split_axis=0, concat_axis=0, axis_index_groups=SCATTER_GROUPS
    )
    piece = lax.dynamic_index_in_dim(
        arrived, (owner_z % 2) * NX + owner_x, axis=0, keepdims=False
    )
    crossed = lax.ppermute(piece, "cand", cand_pairs(lambda x, z: (x, z ^ 2)))
    return jnp.where(owner_z // 2 == z // 2, piece, crossed)


def projection_kernel(kept, place_ref, own_ref, other_ref, rows_ref, *out_refs):
    rows = rows_ref[...]
    core, parity = place_ref[0], place_ref[1]
    for j in range(own_ref.shape[1] // HD // 2):
        block = 2 * j + (parity if kept else 1 - parity)
        lanes = pl.ds(pl.multiple_of(block * HD, HD), HD)
        both = dot_n(rows, jnp.concatenate([own_ref[:, lanes], other_ref[:, lanes]], axis=1))
        if kept:
            out_refs[0][core, j] = both[:, :HD]
            out_refs[0][1 - core, j] = both[:, HD:]
        else:
            out_refs[0][j] = both[:, :HD].astype(jnp.bfloat16)
            out_refs[1][j] = both[:, HD:].astype(jnp.bfloat16)


def project(rows, own, other, kept):
    n = lax.axis_size("tensor") // 2
    count, depth = rows.shape
    place = jnp.stack([lax.axis_index("prompt") % 2, lax.axis_index("tensor") % 2])
    vmem = pl.BlockSpec(memory_space=pltpu.VMEM)
    if kept:
        out_shape = [jax.ShapeDtypeStruct((2, n, count, HD), jnp.float32)]
    else:
        out_shape = [jax.ShapeDtypeStruct((n, count, HD), jnp.bfloat16)] * 2
    return pl.pallas_call(
        lambda *refs: projection_kernel(kept, *refs),
        out_shape=out_shape,
        in_specs=[pl.BlockSpec(memory_space=pltpu.SMEM)] + [vmem] * 3,
        out_specs=[vmem] * len(out_shape),
        compiler_params=pltpu.CompilerParams(vmem_limit_bytes=32 * 1024 * 1024),
        cost_estimate=pl.CostEstimate(
            flops=80 * own.shape[1] * count * depth,
            bytes_accessed=4 * own.size,
            transcendentals=0,
        ),
    )(place.astype(jnp.int32), own, other, rows)


def pair_sums(rows, own, other):
    own_sent, other_sent = project(rows, own, other, kept=False)
    n = lax.axis_size("tensor")
    up = [(t, (t + 1) % n if t % 2 == 0 else t - 1) for t in range(n)]
    down = [(t, (t - 1) % n if t % 2 == 0 else (t + 1) % n) for t in range(n)]
    own_got = lax.ppermute(own_sent, "tensor", up)
    other_got = lax.ppermute(other_sent, "tensor", down)
    (keep,) = project(rows, own, other, kept=True)
    even = lax.axis_index("prompt") % 2 == 0
    got = [jnp.where(even, own_got, other_got), jnp.where(even, other_got, own_got)]
    return keep + jnp.stack(got).astype(jnp.float32)


def exchange(terms):
    cores, n, rows, columns = terms.shape
    groups = [
        [(2 * z + core) * 2 * n + 2 * j + parity for core in range(cores) for j in range(n)]
        for z in range(2)
        for parity in range(2)
    ]
    terms = lax.all_to_all(
        terms.astype(jnp.bfloat16).reshape(cores * n, rows, columns),
        ("prompt", "tensor"),
        split_axis=0,
        concat_axis=0,
        axis_index_groups=groups,
    )
    terms = terms.reshape(cores, n, rows, columns).astype(jnp.float32)
    return terms.sum(axis=1).astype(jnp.bfloat16)


def swap(value, bit):
    return lax.ppermute(value, "prompt", [(p, p ^ bit) for p in range(4)])


def move(value, shift):
    return lax.ppermute(value, "cand", cand_pairs(lambda x, z: (x + shift, z)))


def body(owner_index, suffix_lengths, queries, suffix_kv, prompt_cache, out_weight):
    query_rows = queries[0]
    weights = [out_weight, swap(out_weight, 1)]
    piece = spread_piece(prompt_cache[:, 0, 0], owner_index[0])
    keys_first = (lax.axis_index("cand") % 2 == 0).astype(jnp.int32)
    scalars = jnp.stack([keys_first, suffix_lengths[0, 0]])
    other = lax.ppermute(piece, "cand", cand_pairs(lambda x, z: (x, z ^ 1)))
    left, right = [move(piece, 1)], [move(piece, -1)]
    left.append(move(other, 1))
    right.append(move(other, -1))
    across = [move(right[0], -1), move(left[1], 1)]
    state = attend(scalars, query_rows, [(piece, other)], suffix=suffix_kv[:, 0])
    state = attend(scalars, query_rows, [left, right], state=state)
    attended = attend(scalars, query_rows, [across], state=state, last=True)
    far_rows = swap(attended, 2)
    near_terms = pair_sums(attended, *weights)
    near = exchange(near_terms)
    _, far_rows = lax.optimization_barrier((near_terms, far_rows))
    far_terms, _ = lax.optimization_barrier((pair_sums(far_rows, *weights), near))
    far = exchange(far_terms)
    first = lax.axis_index("prompt") < 2
    return jnp.concatenate([jnp.where(first, near, far), jnp.where(first, far, near)])


def solution(mesh):
    in_specs = (
        P("prompt"),
        P("prompt", "cand"),
        P("prompt", "cand", "tensor"),
        P(None, "prompt", "cand", "tensor"),
        P(None, "prompt", "cand", None, "tensor"),
        P("tensor", "prompt"),
    )
    out_specs = P(None, "cand", ("prompt", "tensor"))
    return jax.shard_map(body, mesh=mesh, in_specs=in_specs, out_specs=out_specs, check_vma=False)
```

```python
import math

import jax
import jax.numpy as jnp
from jax import lax
from jax.experimental import pallas as pl
from jax.experimental.pallas import tpu as pltpu
from jax.sharding import PartitionSpec as P

HD = 128
SUF = 256
NX = 4
NZ = 4
GROUP = 8
CHUNK = 512
EXP2_SCALE = math.log2(math.e) / math.sqrt(HD)
MASKED = -1e30


def cand_pairs(f):
    pairs = []
    for x in range(NX):
        for z in range(NZ):
            tx, tz = f(x, z)
            pairs.append((x * NZ + z, (tx % NX) * NZ + tz))
    return pairs


def ring_pairs(n, shift):
    return [(i, (i + shift) % n) for i in range(n)]


SCATTER_GROUPS = [
    [x * NZ + 2 * pair + zi for zi in range(2) for x in range(NX)] for pair in range(2)
]


def dot_t(a, b):
    return lax.dot_general(a, b, (((1,), (1,)), ((), ())), preferred_element_type=jnp.float32)


def dot_n(a, b):
    return lax.dot_general(a, b, (((1,), (0,)), ((), ())), preferred_element_type=jnp.float32)


def with_ones(values):
    return jnp.concatenate([values, jnp.ones_like(values)], axis=1)


def attention_kernel(n_blocks, has_suffix, has_state, last, heads, scalar_ref, *refs):
    refs = list(refs)
    q_ref = refs.pop(0)
    block_refs = [(refs.pop(0), refs.pop(0)) for _ in range(n_blocks)]
    suffix_ref = refs.pop(0) if has_suffix else None
    state_refs = [refs.pop(0) for _ in range(3)] if has_state else None
    outs = refs
    rows = q_ref.shape[0]
    keys_first = scalar_ref[0] == 1
    keys, values = [], []
    for a, b in block_refs:
        for start in range(0, a.shape[0], CHUNK):
            chunk = pl.ds(start, CHUNK)
            keys.append(jnp.where(keys_first, a[chunk], b[chunk]))
            values.append(with_ones(jnp.where(keys_first, b[chunk], a[chunk])))
    if has_suffix:
        keys.append(suffix_ref[0])
        values.append(with_ones(suffix_ref[1]))
        row = lax.broadcasted_iota(jnp.int32, (rows, rows), 0)
        col = lax.broadcasted_iota(jnp.int32, (rows, rows), 1)
        allowed = (col <= row) & (col < scalar_ref[1])

    def score(lanes):
        query = q_ref[:, lanes]
        scores = [dot_t(query, k) * EXP2_SCALE for k in keys]
        if has_suffix:
            scores[-1] = jnp.where(allowed, scores[-1], MASKED)
        return lanes, scores

    def weigh(lanes, scores):
        row_max = scores[0].max(axis=1, keepdims=True)
        for s in scores[1:]:
            row_max = jnp.maximum(row_max, s.max(axis=1, keepdims=True))
        if has_state:
            old_max = state_refs[1][:, lanes]
            new_max = jnp.maximum(old_max, row_max)
            row_max = new_max[:, :1]
        total = None
        for s, v in zip(scores, values):
            weights = jnp.exp2(s - row_max).astype(jnp.bfloat16)
            part = dot_n(weights, v)
            total = part if total is None else total + part
        acc, denom = total[:, :HD], total[:, HD:]
        if has_state:
            alpha = jnp.exp2(old_max - new_max)
            acc = acc + alpha * state_refs[0][:, lanes]
            denom = denom + alpha * state_refs[2][:, lanes]
        if last:
            outs[0][:, lanes] = (acc / denom).astype(jnp.bfloat16)
        else:
            outs[0][:, lanes] = acc
            outs[1][:, lanes] = jnp.broadcast_to(row_max, (rows, HD))
            outs[2][:, lanes] = denom

    pending = None
    for h in range(heads):
        scored = score(pl.ds(h * HD, HD))
        if pending is not None:
            weigh(*pending)
        pending = scored
    weigh(*pending)


def attend(scalars, query_rows, blocks, suffix=None, state=None, last=False):
    rows, width = query_rows.shape
    heads = width // HD
    operands = [query_rows]
    for block in blocks:
        operands.extend(block)
    key_count = sum(a.shape[0] for a, _ in blocks)
    if suffix is not None:
        operands.append(suffix)
        key_count += suffix.shape[1]
    if state is not None:
        operands.extend(state)
    vmem = pl.BlockSpec(memory_space=pltpu.VMEM)
    if last:
        out_shape = [jax.ShapeDtypeStruct((rows, width), jnp.bfloat16)]
    else:
        out_shape = [jax.ShapeDtypeStruct((rows, width), jnp.float32)] * 3
    out = pl.pallas_call(
        lambda *refs: attention_kernel(
            len(blocks), suffix is not None, state is not None, last, heads, *refs
        ),
        out_shape=out_shape,
        in_specs=[pl.BlockSpec(memory_space=pltpu.SMEM)] + [vmem] * len(operands),
        out_specs=[vmem] * len(out_shape),
        compiler_params=pltpu.CompilerParams(vmem_limit_bytes=40 * 1024 * 1024),
        cost_estimate=pl.CostEstimate(
            flops=8 * rows * heads * key_count * HD,
            bytes_accessed=2**22,
            transcendentals=rows * heads * key_count,
        ),
    )(scalars, *operands)
    return out[0] if last else out


def spread_piece(prompt_kv, owner):
    me = lax.axis_index("cand")
    z = me % NZ
    owner_x, owner_z = owner // NZ, owner % NZ
    pieces = prompt_kv.reshape(GROUP, -1, HD)
    arrived = lax.all_to_all(
        pieces, "cand", split_axis=0, concat_axis=0, axis_index_groups=SCATTER_GROUPS
    )
    piece = lax.dynamic_index_in_dim(
        arrived, (owner_z % 2) * NX + owner_x, axis=0, keepdims=False
    )
    crossed = lax.ppermute(piece, "cand", cand_pairs(lambda x, z: (x, z ^ 2)))
    return jnp.where(owner_z // 2 == z // 2, piece, crossed)


def projection_kernel(kept, place_ref, own_ref, other_ref, rows_ref, *out_refs):
    rows = rows_ref[...]
    core, parity = place_ref[0], place_ref[1]
    for j in range(own_ref.shape[1] // HD // 2):
        block = 2 * j + (parity if kept else 1 - parity)
        lanes = pl.ds(pl.multiple_of(block * HD, HD), HD)
        both = dot_n(rows, jnp.concatenate([own_ref[:, lanes], other_ref[:, lanes]], axis=1))
        if kept:
            out_refs[0][core, j] = both[:, :HD]
            out_refs[0][1 - core, j] = both[:, HD:]
        else:
            out_refs[0][j] = both[:, :HD].astype(jnp.bfloat16)
            out_refs[1][j] = both[:, HD:].astype(jnp.bfloat16)


def project(rows, own, other, kept):
    n = lax.axis_size("tensor") // 2
    count, depth = rows.shape
    place = jnp.stack([lax.axis_index("prompt") % 2, lax.axis_index("tensor") % 2])
    vmem = pl.BlockSpec(memory_space=pltpu.VMEM)
    if kept:
        out_shape = [jax.ShapeDtypeStruct((2, n, count, HD), jnp.float32)]
    else:
        out_shape = [jax.ShapeDtypeStruct((n, count, HD), jnp.bfloat16)] * 2
    return pl.pallas_call(
        lambda *refs: projection_kernel(kept, *refs),
        out_shape=out_shape,
        in_specs=[pl.BlockSpec(memory_space=pltpu.SMEM)] + [vmem] * 3,
        out_specs=[vmem] * len(out_shape),
        compiler_params=pltpu.CompilerParams(vmem_limit_bytes=32 * 1024 * 1024),
        cost_estimate=pl.CostEstimate(
            flops=80 * own.shape[1] * count * depth,
            bytes_accessed=4 * own.size,
            transcendentals=0,
        ),
    )(place.astype(jnp.int32), own, other, rows)


def pair_sums(rows, own, other):
    own_sent, other_sent = project(rows, own, other, kept=False)
    n = lax.axis_size("tensor")
    up = [(t, (t + 1) % n if t % 2 == 0 else t - 1) for t in range(n)]
    down = [(t, (t - 1) % n if t % 2 == 0 else (t + 1) % n) for t in range(n)]
    own_got = lax.ppermute(own_sent, "tensor", up)
    other_got = lax.ppermute(other_sent, "tensor", down)
    (keep,) = project(rows, own, other, kept=True)
    even = lax.axis_index("prompt") % 2 == 0
    got = [jnp.where(even, own_got, other_got), jnp.where(even, other_got, own_got)]
    return keep + jnp.stack(got).astype(jnp.float32)


def exchange(terms):
    cores, n, rows, columns = terms.shape
    groups = [
        [(2 * z + core) * 2 * n + 2 * j + parity for core in range(cores) for j in range(n)]
        for z in range(2)
        for parity in range(2)
    ]
    terms = lax.all_to_all(
        terms.astype(jnp.bfloat16).reshape(cores * n, rows, columns),
        ("prompt", "tensor"),
        split_axis=0,
        concat_axis=0,
        axis_index_groups=groups,
    )
    return terms.reshape(cores, n, rows, columns)


def add_up(terms):
    return terms.astype(jnp.float32).sum(axis=1).astype(jnp.bfloat16)


def swap(value, bit):
    return lax.ppermute(value, "prompt", [(p, p ^ bit) for p in range(4)])


def move(value, shift):
    return lax.ppermute(value, "cand", cand_pairs(lambda x, z: (x + shift, z)))


def body(owner_index, suffix_lengths, queries, suffix_kv, prompt_cache, out_weight):
    query_rows = queries[0]
    weights = [out_weight, swap(out_weight, 1)]
    piece = spread_piece(prompt_cache[:, 0, 0], owner_index[0])
    keys_first = (lax.axis_index("cand") % 2 == 0).astype(jnp.int32)
    scalars = jnp.stack([keys_first, suffix_lengths[0, 0]])
    other = lax.ppermute(piece, "cand", cand_pairs(lambda x, z: (x, z ^ 1)))
    left, right = [move(piece, 1)], [move(piece, -1)]
    left.append(move(other, 1))
    right.append(move(other, -1))
    across = [move(right[0], -1), move(left[1], 1)]
    state = attend(scalars, query_rows, [(piece, other)], suffix=suffix_kv[:, 0])
    state = attend(scalars, query_rows, [left, right], state=state)
    attended = attend(scalars, query_rows, [across], state=state, last=True)
    far_rows = swap(attended, 2)
    near_terms = pair_sums(attended, *weights)
    near = exchange(near_terms)
    _, far_rows = lax.optimization_barrier((near_terms, far_rows))
    far_terms, near = lax.optimization_barrier((pair_sums(far_rows, *weights), near))
    far = add_up(exchange(far_terms))
    near = add_up(near)
    first = lax.axis_index("prompt") < 2
    return jnp.concatenate([jnp.where(first, near, far), jnp.where(first, far, near)])


def solution(mesh):
    in_specs = (
        P("prompt"),
        P("prompt", "cand"),
        P("prompt", "cand", "tensor"),
        P(None, "prompt", "cand", "tensor"),
        P(None, "prompt", "cand", None, "tensor"),
        P("tensor", "prompt"),
    )
    out_specs = P(None, "cand", ("prompt", "tensor"))
    return jax.shard_map(body, mesh=mesh, in_specs=in_specs, out_specs=out_specs, check_vma=False)
```

```python
import math

import jax
import jax.numpy as jnp
from jax import lax
from jax.experimental import pallas as pl
from jax.experimental.pallas import tpu as pltpu
from jax.sharding import PartitionSpec as P

HD = 128
SUF = 256
NX = 4
NZ = 4
GROUP = 8
CHUNK = 512
EXP2_SCALE = math.log2(math.e) / math.sqrt(HD)
MASKED = -1e30


def cand_pairs(f):
    pairs = []
    for x in range(NX):
        for z in range(NZ):
            tx, tz = f(x, z)
            pairs.append((x * NZ + z, (tx % NX) * NZ + tz))
    return pairs


def ring_pairs(n, shift):
    return [(i, (i + shift) % n) for i in range(n)]


SCATTER_GROUPS = [
    [x * NZ + 2 * pair + zi for zi in range(2) for x in range(NX)] for pair in range(2)
]


def dot_t(a, b):
    return lax.dot_general(a, b, (((1,), (1,)), ((), ())), preferred_element_type=jnp.float32)


def dot_n(a, b):
    return lax.dot_general(a, b, (((1,), (0,)), ((), ())), preferred_element_type=jnp.float32)


def with_ones(values):
    return jnp.concatenate([values, jnp.ones_like(values)], axis=1)


def attention_kernel(n_blocks, has_suffix, has_state, last, heads, scalar_ref, *refs):
    refs = list(refs)
    q_ref = refs.pop(0)
    block_refs = [(refs.pop(0), refs.pop(0)) for _ in range(n_blocks)]
    suffix_ref = refs.pop(0) if has_suffix else None
    state_refs = [refs.pop(0) for _ in range(3)] if has_state else None
    outs = refs
    rows = q_ref.shape[0]
    keys_first = scalar_ref[0] == 1
    keys, values = [], []
    for a, b in block_refs:
        for start in range(0, a.shape[0], CHUNK):
            chunk = pl.ds(start, CHUNK)
            keys.append(jnp.where(keys_first, a[chunk], b[chunk]))
            values.append(with_ones(jnp.where(keys_first, b[chunk], a[chunk])))
    if has_suffix:
        keys.append(suffix_ref[0])
        values.append(with_ones(suffix_ref[1]))
        row = lax.broadcasted_iota(jnp.int32, (rows, rows), 0)
        col = lax.broadcasted_iota(jnp.int32, (rows, rows), 1)
        allowed = (col <= row) & (col < scalar_ref[1])

    def score(lanes):
        query = q_ref[:, lanes]
        scores = [dot_t(query, k) * EXP2_SCALE for k in keys]
        if has_suffix:
            scores[-1] = jnp.where(allowed, scores[-1], MASKED)
        return lanes, scores

    def weigh(lanes, scores):
        row_max = scores[0].max(axis=1, keepdims=True)
        for s in scores[1:]:
            row_max = jnp.maximum(row_max, s.max(axis=1, keepdims=True))
        if has_state:
            old_max = state_refs[1][:, lanes]
            new_max = jnp.maximum(old_max, row_max)
            row_max = new_max[:, :1]
        total = None
        for s, v in zip(scores, values):
            weights = jnp.exp2(s - row_max).astype(jnp.bfloat16)
            part = dot_n(weights, v)
            total = part if total is None else total + part
        acc, denom = total[:, :HD], total[:, HD:]
        if has_state:
            alpha = jnp.exp2(old_max - new_max)
            acc = acc + alpha * state_refs[0][:, lanes]
            denom = denom + alpha * state_refs[2][:, lanes]
        if last:
            outs[0][:, lanes] = (acc / denom).astype(jnp.bfloat16)
        else:
            outs[0][:, lanes] = acc
            outs[1][:, lanes] = jnp.broadcast_to(row_max, (rows, HD))
            outs[2][:, lanes] = denom

    pending = None
    for h in range(heads):
        scored = score(pl.ds(h * HD, HD))
        if pending is not None:
            weigh(*pending)
        pending = scored
    weigh(*pending)


def attend(scalars, query_rows, blocks, suffix=None, state=None, last=False):
    rows, width = query_rows.shape
    heads = width // HD
    operands = [query_rows]
    for block in blocks:
        operands.extend(block)
    key_count = sum(a.shape[0] for a, _ in blocks)
    if suffix is not None:
        operands.append(suffix)
        key_count += suffix.shape[1]
    if state is not None:
        operands.extend(state)
    vmem = pl.BlockSpec(memory_space=pltpu.VMEM)
    if last:
        out_shape = [jax.ShapeDtypeStruct((rows, width), jnp.bfloat16)]
    else:
        out_shape = [jax.ShapeDtypeStruct((rows, width), jnp.float32)] * 3
    out = pl.pallas_call(
        lambda *refs: attention_kernel(
            len(blocks), suffix is not None, state is not None, last, heads, *refs
        ),
        out_shape=out_shape,
        in_specs=[pl.BlockSpec(memory_space=pltpu.SMEM)] + [vmem] * len(operands),
        out_specs=[vmem] * len(out_shape),
        compiler_params=pltpu.CompilerParams(vmem_limit_bytes=40 * 1024 * 1024),
        cost_estimate=pl.CostEstimate(
            flops=8 * rows * heads * key_count * HD,
            bytes_accessed=2**22,
            transcendentals=rows * heads * key_count,
        ),
    )(scalars, *operands)
    return out[0] if last else out


def spread_piece(prompt_kv, owner, ready):
    me = lax.axis_index("cand")
    z = me % NZ
    owner_x, owner_z = owner // NZ, owner % NZ
    pieces = prompt_kv.reshape(GROUP, -1, HD)
    arrived = lax.all_to_all(
        pieces, "cand", split_axis=0, concat_axis=0, axis_index_groups=SCATTER_GROUPS
    )
    piece = lax.dynamic_index_in_dim(
        arrived, (owner_z % 2) * NX + owner_x, axis=0, keepdims=False
    )
    crossed = lax.ppermute(piece, "cand", cand_pairs(lambda x, z: (x, z ^ 2)))
    crossed, ready = lax.optimization_barrier((crossed, ready))
    return jnp.where(owner_z // 2 == z // 2, piece, crossed), ready


def interleave_kernel(own_ref, other_ref, out_ref):
    for i in range(own_ref.shape[1] // HD):
        out_ref[:, 2 * i * HD : (2 * i + 1) * HD] = own_ref[:, i * HD : (i + 1) * HD]
        out_ref[:, (2 * i + 1) * HD : (2 * i + 2) * HD] = other_ref[:, i * HD : (i + 1) * HD]


def interleave(own, other):
    vmem = pl.BlockSpec(memory_space=pltpu.VMEM)
    return pl.pallas_call(
        interleave_kernel,
        out_shape=jax.ShapeDtypeStruct((own.shape[0], 2 * own.shape[1]), own.dtype),
        in_specs=[vmem] * 2,
        out_specs=vmem,
        compiler_params=pltpu.CompilerParams(vmem_limit_bytes=16 * 1024 * 1024),
        cost_estimate=pl.CostEstimate(flops=0, bytes_accessed=8 * own.size, transcendentals=0),
    )(own, other)


def projection_kernel(kept, place_ref, weight_ref, rows_ref, *out_refs):
    rows = rows_ref[...]
    core, parity = place_ref[0], place_ref[1]
    for j in range(weight_ref.shape[1] // HD // 4):
        block = 2 * j + (parity if kept else 1 - parity)
        lanes = pl.ds(pl.multiple_of(block * 2 * HD, 2 * HD), 2 * HD)
        both = dot_n(rows, weight_ref[:, lanes])
        if kept:
            out_refs[0][core, j] = both[:, :HD]
            out_refs[0][1 - core, j] = both[:, HD:]
        else:
            out_refs[0][j] = both[:, :HD].astype(jnp.bfloat16)
            out_refs[1][j] = both[:, HD:].astype(jnp.bfloat16)


def project(rows, weight, kept):
    n = lax.axis_size("tensor") // 2
    count, depth = rows.shape
    place = jnp.stack([lax.axis_index("prompt") % 2, lax.axis_index("tensor") % 2])
    vmem = pl.BlockSpec(memory_space=pltpu.VMEM)
    if kept:
        out_shape = [jax.ShapeDtypeStruct((2, n, count, HD), jnp.float32)]
    else:
        out_shape = [jax.ShapeDtypeStruct((n, count, HD), jnp.bfloat16)] * 2
    return pl.pallas_call(
        lambda *refs: projection_kernel(kept, *refs),
        out_shape=out_shape,
        in_specs=[pl.BlockSpec(memory_space=pltpu.SMEM)] + [vmem] * 2,
        out_specs=[vmem] * len(out_shape),
        compiler_params=pltpu.CompilerParams(vmem_limit_bytes=32 * 1024 * 1024),
        cost_estimate=pl.CostEstimate(
            flops=40 * weight.shape[1] * count * depth,
            bytes_accessed=2 * weight.size,
            transcendentals=0,
        ),
    )(place.astype(jnp.int32), weight, rows)


def pair_sums(rows, weight):
    own_sent, other_sent = project(rows, weight, kept=False)
    n = lax.axis_size("tensor")
    up = [(t, (t + 1) % n if t % 2 == 0 else t - 1) for t in range(n)]
    down = [(t, (t - 1) % n if t % 2 == 0 else (t + 1) % n) for t in range(n)]
    own_got = lax.ppermute(own_sent, "tensor", up)
    other_got = lax.ppermute(other_sent, "tensor", down)
    (keep,) = project(rows, weight, kept=True)
    even = lax.axis_index("prompt") % 2 == 0
    got = [jnp.where(even, own_got, other_got), jnp.where(even, other_got, own_got)]
    return keep + jnp.stack(got).astype(jnp.float32)


def exchange(terms):
    cores, n, rows, columns = terms.shape
    groups = [
        [(2 * z + core) * 2 * n + 2 * j + parity for core in range(cores) for j in range(n)]
        for z in range(2)
        for parity in range(2)
    ]
    terms = lax.all_to_all(
        terms.astype(jnp.bfloat16).reshape(cores * n, rows, columns),
        ("prompt", "tensor"),
        split_axis=0,
        concat_axis=0,
        axis_index_groups=groups,
    )
    return terms.reshape(cores, n, rows, columns)


def add_up(terms):
    return terms.astype(jnp.float32).sum(axis=1).astype(jnp.bfloat16)


def swap(value, bit):
    return lax.ppermute(value, "prompt", [(p, p ^ bit) for p in range(4)])


def move(value, shift):
    return lax.ppermute(value, "cand", cand_pairs(lambda x, z: (x + shift, z)))


def body(owner_index, suffix_lengths, queries, suffix_kv, prompt_cache, out_weight):
    query_rows = queries[0]
    weight = interleave(out_weight, swap(out_weight, 1))
    piece, weight = spread_piece(prompt_cache[:, 0, 0], owner_index[0], weight)
    keys_first = (lax.axis_index("cand") % 2 == 0).astype(jnp.int32)
    scalars = jnp.stack([keys_first, suffix_lengths[0, 0]])
    other = lax.ppermute(piece, "cand", cand_pairs(lambda x, z: (x, z ^ 1)))
    left, right = [move(piece, 1)], [move(piece, -1)]
    left.append(move(other, 1))
    right.append(move(other, -1))
    across = [move(right[0], -1), move(left[1], 1)]
    state = attend(scalars, query_rows, [(piece, other)], suffix=suffix_kv[:, 0])
    state = attend(scalars, query_rows, [left, right], state=state)
    attended = attend(scalars, query_rows, [across], state=state, last=True)
    far_rows = swap(attended, 2)
    near_terms = pair_sums(attended, weight)
    near = exchange(near_terms)
    _, far_rows = lax.optimization_barrier((near_terms, far_rows))
    far_terms, near = lax.optimization_barrier((pair_sums(far_rows, weight), near))
    far = add_up(exchange(far_terms))
    near = add_up(near)
    first = lax.axis_index("prompt") < 2
    return jnp.concatenate([jnp.where(first, near, far), jnp.where(first, far, near)])


def solution(mesh):
    in_specs = (
        P("prompt"),
        P("prompt", "cand"),
        P("prompt", "cand", "tensor"),
        P(None, "prompt", "cand", "tensor"),
        P(None, "prompt", "cand", None, "tensor"),
        P("tensor", "prompt"),
    )
    out_specs = P(None, "cand", ("prompt", "tensor"))
    return jax.shard_map(body, mesh=mesh, in_specs=in_specs, out_specs=out_specs, check_vma=False)
```
